128 devices in a mesh: member: 4 (over z_lo, core), slab: 32 (over x, z_hi, y).
Axes of the slice: x: 4, y: 4, z: 4 (z_hi: 2, z_lo: 2; z = z_hi * 2 + z_lo), core: 2. Of those that a mesh axis runs over, the one named last changes fastest.
Arguments:
- structure: float32 [8, 256, 256, 256], P('member', 'slab'), may hold values from 0.02 to 0.98
- upstream: float32 [8, 256, 256, 256], P('member', 'slab'), may hold values from -6 to 6
- noise: float32 [2, 8, 256, 256, 256], P(None, 'member', None, 'slab'), may hold values from -6 to 6
- density: float32 [256, 256, 256], P('member', 'slab'), may hold values from 0.1 to 10
Outputs:
- density_grad: float32 [256, 256, 256], P('member', 'slab')
The draws below stay inside these ranges and needn't reach their ends.
All inputs are finite; a program needn't handle non-finite values.
Results may differ from the reference program's by a relative error of at most 0.0001.
Values sent between devices are 32-bit elements; how exact they have to be, the bound alone decides.
No kernel may reach another device: no remote copies, remote signals or barrier semaphores. Data moves between devices by JAX's collectives and lax.ppermute only.
A program may use at most 128 MiB of HBM per device.

```python
import math
import jax
import jax.numpy as jnp

GRID = 256
MEMBERS = 8


def spiked(values, key, source, target, shards_of, factor):
    owner, partner = [(jnp.arange(values.shape[position]) // (values.shape[position] // shards_of)).reshape([-1 if axis == position else 1 for axis in range(values.ndim)]) for position in (source, target)]
    chosen = jax.random.permutation(key, shards_of)[partner]
    strong = (owner == chosen) | (owner == (partner + shards_of // 2) % shards_of)
    return jnp.where(strong, factor * values, values)


def block_scale(rng, shape, cuts, smallest, high):
    def one(position, shards_of):
        draws = jax.random.uniform(jax.random.fold_in(jax.random.fold_in(rng, 6), position), (shards_of,), jnp.float32, smallest / len(cuts), high / len(cuts))
        return jnp.repeat(jnp.exp(draws), shape[position] // shards_of).reshape((-1,) + (1,) * (len(shape) - position - 1))

    loudness = one(*cuts[0])
    for cut in cuts[1:]:
        loudness = loudness * one(*cut)
    return loudness


def gaussian(stream_key, shape, scale, limit, shards=(), kind=jnp.bfloat16):
    drawn = jax.random.normal(stream_key, shape, jnp.float32) * scale
    if len(shards) > 0:
        drawn = block_scale(stream_key, shape, shards, -0.22, 0.18) * drawn
    return jnp.clip(drawn, min=-limit, max=limit).astype(kind)


def noise_with(key, dims, width, reach, shards, heavy, kind=jnp.bfloat16):
    values = width * jax.random.normal(key, dims, jnp.float32)
    if shards:
        values = values * block_scale(key, dims, shards, -0.22, 0.18)
    return jnp.clip(spiked(values, jax.random.fold_in(key, 3), *heavy), -reach, reach).astype(kind)


def setup_inputs(seed: int = 0) -> dict:
    key_of = jax.random.split(jax.random.key(seed), 5)
    structure = jnp.clip(0.02 + 0.96000002 * jax.random.uniform(key_of[0], (MEMBERS, GRID, GRID, GRID), jnp.float32) ** block_scale(key_of[0], (MEMBERS, GRID, GRID, GRID), ((0, 4), (1, 32)), -0.2, 0.2), 0.02, 0.98)
    upstream = gaussian(key_of[1], (MEMBERS, GRID, GRID, GRID), 1.0, 6.0, ((0, 4), (1, 32)), jnp.float32)
    noise = noise_with(key_of[2], (2, MEMBERS, GRID, GRID, GRID), 1.0, 6.0, ((1, 4), (3, 32)), (1, 2, 4, 2.0), jnp.float32)
    density = jnp.clip(jnp.exp(math.log(10.0) - 4.6051702 * jax.random.uniform(key_of[3], (GRID, GRID, GRID), jnp.float32) ** block_scale(key_of[3], (GRID, GRID, GRID), ((0, 4), (1, 32)), -0.2, 0.2)), 0.1, 10.0)
    return dict(structure=structure, upstream=upstream, noise=noise, density=density)


sigmoid_slope = 8.0

def reference(structure, upstream, noise, density):
    summed = jnp.zeros((GRID, GRID, GRID), jnp.float32)
    for member in range(MEMBERS):
        field_grad = upstream[member] * sigmoid_slope * structure[member] * (1.0 - structure[member])
        spectrum = jnp.fft.fftn(field_grad, norm='ortho')
        summed = summed + noise[0, member] * jnp.real(spectrum) + noise[1, member] * jnp.imag(spectrum)
    return summed / (2.0 * jnp.sqrt(density))
```

```python
import math

import jax
import jax.numpy as jnp
from jax import lax
from jax.sharding import PartitionSpec as P

sigmoid_slope = 8.0


def dft_tables(length_grid):
    indices = jnp.arange(length_grid, dtype=jnp.int32)
    products = indices[:, None] * indices[None, :] % length_grid
    angles = products.astype(jnp.float32) * (2.0 * math.pi / length_grid)
    factor_norm = 1.0 / math.sqrt(length_grid)
    return (jnp.cos(angles) * factor_norm, jnp.sin(angles) * factor_norm)


def contract(form, values, table):
    return jnp.einsum(
        form, values, table, precision=lax.Precision.HIGH, preferred_element_type=jnp.float32
    )


def swap(values, axis, flip):
    return lax.ppermute(values, axis, [(i, i ^ flip) for i in range(4)])


def sum_over_members(local_sum):
    index = lax.axis_index("member")
    z_lo, core = index // 2, index % 2
    blocks = local_sum.reshape((2, 2, 64) + local_sum.shape[1:])
    keep = lax.dynamic_index_in_dim(blocks, core, 1, keepdims=False)
    give = lax.dynamic_index_in_dim(blocks, 1 - core, 1, keepdims=False)
    chip = keep + swap(give, "member", 1)
    mine = lax.dynamic_index_in_dim(chip, z_lo, 0, keepdims=False)
    theirs = lax.dynamic_index_in_dim(chip, 1 - z_lo, 0, keepdims=False)
    return mine + swap(theirs, "member", 2)


def body(structure, upstream, noise, density):
    length_grid = structure.shape[-1]
    cosine_table, sine_table = dft_tables(length_grid)
    field_grad = upstream * sigmoid_slope * structure * (1.0 - structure)
    after_z_real = contract("mxyz,zk->mxyk", field_grad, cosine_table)
    after_z_imag = -contract("mxyz,zk->mxyk", field_grad, sine_table)
    after_y_real = contract("mxyz,yk->mxkz", after_z_real, cosine_table) + contract(
        "mxyz,yk->mxkz", after_z_imag, sine_table
    )
    after_y_imag = contract("mxyz,yk->mxkz", after_z_imag, cosine_table) - contract(
        "mxyz,yk->mxkz", after_z_real, sine_table
    )
    planes = jnp.stack((after_y_real, after_y_imag))
    planes = planes.reshape((2,) + structure.shape[:2] + (32, 8, length_grid))
    planes = jnp.transpose(planes, (3, 0, 1, 2, 4, 5))
    received = lax.all_to_all(planes, "slab", split_axis=0, concat_axis=0, tiled=True)
    received, noise, density = lax.optimization_barrier((received, noise, density))
    slab_block = jnp.transpose(received, (1, 2, 0, 3, 4, 5)).reshape(
        (2, structure.shape[0], length_grid, 8, length_grid)
    )
    real_part = slab_block[0]
    imag_part = slab_block[1]
    out_real = contract("mxyz,xk->mkyz", real_part, cosine_table) + contract(
        "mxyz,xk->mkyz", imag_part, sine_table
    )
    out_imag = contract("mxyz,xk->mkyz", imag_part, cosine_table) - contract(
        "mxyz,xk->mkyz", real_part, sine_table
    )
    local_sum = jnp.sum(noise[0] * out_real + noise[1] * out_imag, axis=0)
    return sum_over_members(local_sum) / (2.0 * jnp.sqrt(density))


def solution(mesh):
    in_specs = (
        P("member", "slab", None, None),
        P("member", "slab", None, None),
        P(None, "member", None, "slab", None),
        P("member", "slab", None),
    )
    out_specs = P("member", "slab", None)
    return jax.shard_map(body, mesh=mesh, in_specs=in_specs, out_specs=out_specs, check_vma=False)
```

```python
import math

import jax
import jax.numpy as jnp
import ml_dtypes
import numpy as np
from jax import lax
from jax.experimental import pallas as pl
from jax.experimental.pallas import tpu as pltpu
from jax.sharding import PartitionSpec as P

sigmoid_slope = 8.0
grid_length = 256
half = grid_length // 2
devices_slab = 32
devices_member = 4


def waves(rows, columns):
    angles = (np.outer(rows, columns) % grid_length) * (2.0 * math.pi / grid_length)
    return np.cos(angles) / 16.0, -np.sin(angles) / 16.0


def split_table(table):
    high = table.astype(np.float32).astype(ml_dtypes.bfloat16)
    low = (table - high.astype(np.float64)).astype(np.float32).astype(ml_dtypes.bfloat16)
    return high, low


def along_z_table():
    real, imag = waves(np.arange(grid_length), np.arange(grid_length))
    high, low = split_table(np.concatenate((real, imag), axis=1))
    return np.concatenate((high, high, low), axis=0)


def halves_table(order):
    tables = []
    for parity in range(2):
        real, imag = waves(order, np.arange(parity, grid_length, 2))
        full = np.concatenate(
            (np.concatenate((real, -imag), axis=1), np.concatenate((imag, real), axis=1)), axis=0
        )
        high, low = split_table(full)
        tables.append(np.concatenate((high, low, high), axis=1))
    return np.stack(tables)


def split_rows(values):
    high = values.astype(jnp.bfloat16)
    low = (values - high.astype(jnp.float32)).astype(jnp.bfloat16)
    return jnp.concatenate((high, high, low), axis=0)


def dot(left, right):
    return jnp.dot(left, right, preferred_element_type=jnp.float32)


def planes_kernel(left_ref, right_ref, left_up_ref, right_up_ref, z_ref, y_ref, out_ref):
    def field_grad(parity, structure_ref, upstream_ref):
        rows = pl.ds(parity, half, stride=2)
        structure = structure_ref[0, 0, rows, :]
        return upstream_ref[0, 0, rows, :] * sigmoid_slope * structure * (1.0 - structure)

    field = jnp.concatenate(
        [
            jnp.concatenate(
                (
                    field_grad(parity, left_ref, left_up_ref),
                    field_grad(parity, right_ref, right_up_ref),
                ),
                axis=1,
            )
            for parity in range(2)
        ],
        axis=0,
    )
    high = field.astype(jnp.bfloat16)
    low = (field - high.astype(jnp.float32)).astype(jnp.bfloat16)
    after_z = dot(jnp.concatenate((high, low, high), axis=1), z_ref[...])
    sums = []
    for parity in range(2):
        rows = after_z[parity * half : (parity + 1) * half]
        stacked = jnp.concatenate((rows[:, :grid_length], rows[:, grid_length:]), axis=0)
        sums.append(dot(y_ref[parity], split_rows(stacked)))
    below, above = sums[0] + sums[1], sums[0] - sums[1]
    for part in range(2):
        rows = slice(part * half, (part + 1) * half)
        out_ref[:16, part, 0, 0] = below[rows].reshape(16, 8, grid_length)
        out_ref[16:, part, 0, 0] = above[rows].reshape(16, 8, grid_length)


def planes(structure, upstream):
    members, depth = structure.shape[:2]
    blocks = [
        pl.BlockSpec((1, 1, grid_length, 128), lambda m, x, side=side: (m, x, 0, side))
        for side in range(2)
    ]
    return pl.pallas_call(
        planes_kernel,
        out_shape=jax.ShapeDtypeStruct(
            (devices_slab, 2, members, depth, 8, grid_length), jnp.float32
        ),
        grid=(members, depth),
        in_specs=[
            *blocks,
            *blocks,
            pl.BlockSpec((768, 512), lambda m, x: (0, 0)),
            pl.BlockSpec((2, 256, 768), lambda m, x: (0, 0, 0)),
        ],
        out_specs=pl.BlockSpec(
            (devices_slab, 2, 1, 1, 8, grid_length), lambda m, x: (0, 0, m, x, 0, 0)
        ),
        compiler_params=pltpu.CompilerParams(vmem_limit_bytes=32 * 1024 * 1024),
        name="planes",
    )(structure, structure, upstream, upstream, along_z_table(), halves_table(np.arange(half)))


def sums_kernel(place_ref, real_ref, imag_ref, noise_ref, x_ref, out_ref):
    first = pl.program_id(1) == 0
    z_lo, core = place_ref[0], place_ref[1]
    real_ref = real_ref.reshape(2048, 128)
    imag_ref = imag_ref.reshape(2048, 128)
    for pair in range(4):
        spectra = []
        for parity in range(2):
            stacked = jnp.concatenate(
                [
                    jnp.concatenate(
                        [
                            ref[pl.ds(parity * 8 + 2 * pair + side, half, stride=16), :]
                            for side in range(2)
                        ],
                        axis=1,
                    )
                    for ref in (real_ref, imag_ref)
                ],
                axis=0,
            )
            spectra.append(dot(x_ref[parity], split_rows(stacked)))
        for z, spectrum in enumerate((spectra[0] + spectra[1], spectra[0] - spectra[1])):
            for h in range(2):
                block = jnp.bitwise_xor(z_lo, z) * 2 + jnp.bitwise_xor(core, 1 - h)
                for side in range(2):
                    k = 2 * pair + side
                    lanes = slice(side * 128, (side + 1) * 128)
                    rows = pl.ds(k, 64, stride=8)
                    value = (
                        noise_ref[0, 0, block, rows, :] * spectrum[h * 64 : h * 64 + 64, lanes]
                        + noise_ref[1, 0, block, rows, :]
                        * spectrum[half + h * 64 : half + h * 64 + 64, lanes]
                    )
                    before = jnp.where(first, 0.0, out_ref[h, z, k])
                    out_ref[h, z, k] = before + value


def sums(received, noise, x_table, place):
    members = received.shape[2]
    parts = [
        pl.BlockSpec(
            (devices_slab, 1, 1, 64, 128), lambda z, m, p, part=part: (0, part, m, 0, z)
        )
        for part in range(2)
    ]
    return pl.pallas_call(
        sums_kernel,
        out_shape=jax.ShapeDtypeStruct((2, 2, 8, 64, grid_length), jnp.float32),
        grid_spec=pltpu.PrefetchScalarGridSpec(
            num_scalar_prefetch=1,
            grid=(2, members),
            in_specs=parts
            + [
                pl.BlockSpec((2, 1, 4, 512, 128), lambda z, m, p: (0, m, 0, 0, z)),
                pl.BlockSpec((2, 256, 768), lambda z, m, p: (0, 0, 0)),
            ],
            out_specs=pl.BlockSpec((2, 2, 8, 64, 128), lambda z, m, p: (0, 0, 0, 0, z)),
        ),
        compiler_params=pltpu.CompilerParams(vmem_limit_bytes=48 * 1024 * 1024),
        name="sums",
    )(
        place,
        received.reshape(devices_slab, 2, members, 64, grid_length),
        received.reshape(devices_slab, 2, members, 64, grid_length),
        noise.reshape(2, members, 4, 512, grid_length),
        x_table,
    )


def swap(values, flip):
    return lax.ppermute(values, "member", [(i, i ^ flip) for i in range(devices_member)])


def body(structure, upstream, noise, density):
    index = lax.axis_index("member")
    z_lo, core = index // 2, index % 2
    low, high = np.arange(64), np.arange(64, 128)
    x_tables = np.stack(
        [
            halves_table(np.concatenate(order)).astype(np.float32)
            for order in ((high, low), (low, high))
        ]
    ).astype(ml_dtypes.bfloat16)
    signs = jnp.stack((jnp.float32(1), 1.0 - 2.0 * z_lo.astype(jnp.float32)))
    x_table = jnp.where(core == 0, x_tables[0], x_tables[1]) * signs[:, None, None].astype(
        jnp.bfloat16
    )
    place = jnp.stack((z_lo, core)).astype(jnp.int32)
    sent = planes(structure, upstream)
    sent, x_table, place = lax.optimization_barrier((sent, x_table, place))
    received = lax.all_to_all(sent, "slab", split_axis=0, concat_axis=0, tiled=True)
    received, noise, density, x_table, place = lax.optimization_barrier(
        (received, noise, density, x_table, place)
    )
    partial = sums(received, noise, x_table, place)
    on_chip = partial[1] + swap(partial[0], 1)
    total = on_chip[0] + swap(on_chip[1], 2)
    return jnp.transpose(total, (1, 0, 2)) / (2.0 * jnp.sqrt(density))


def solution(mesh):
    in_specs = (
        P("member", "slab", None, None),
        P("member", "slab", None, None),
        P(None, "member", None, "slab", None),
        P("member", "slab", None),
    )
    out_specs = P("member", "slab", None)
    return jax.shard_map(body, mesh=mesh, in_specs=in_specs, out_specs=out_specs, check_vma=False)
```

```python
import functools
import math

import jax
import jax.numpy as jnp
import ml_dtypes
import numpy as np
from jax import lax
from jax.experimental import pallas as pl
from jax.experimental.pallas import tpu as pltpu
from jax.sharding import PartitionSpec as P

sigmoid_slope = 8.0
grid_length = 256
half = grid_length // 2
devices_slab = 32
devices_member = 4


def waves(rows, columns):
    angles = (np.outer(rows, columns) % grid_length) * (2.0 * math.pi / grid_length)
    return np.cos(angles) / 16.0, -np.sin(angles) / 16.0


def split_table(table):
    high = table.astype(np.float32).astype(ml_dtypes.bfloat16)
    low = (table - high.astype(np.float64)).astype(np.float32).astype(ml_dtypes.bfloat16)
    return high, low


def along_z_table():
    real, imag = waves(np.arange(grid_length), np.arange(grid_length))
    high, low = split_table(np.concatenate((real, imag), axis=1))
    return np.concatenate((high, low), axis=0)


def stacked_table(real, imag):
    full = np.concatenate(
        (np.concatenate((real, -imag), axis=1), np.concatenate((imag, real), axis=1)), axis=0
    )
    return np.concatenate(split_table(full), axis=1)


def along_y_table():
    return np.stack(
        [
            stacked_table(*waves(np.arange(half), np.arange(parity, grid_length, 2)))
            for parity in range(2)
        ]
    )


def along_x_table():
    tables = []
    for core in range(2):
        order = np.concatenate(
            [np.arange(32) + 32 * (2 * z + c) for c in (1 - core, core) for z in range(2)]
        )
        tables.append(
            np.stack(
                [stacked_table(*waves(2 * order + parity, np.arange(half))) for parity in range(2)]
            )
        )
    return np.stack(tables)


def dot(left, right):
    return jnp.dot(left, right, preferred_element_type=jnp.float32)


def halve(values):
    high = values.astype(jnp.bfloat16)
    return high, (values - high.astype(jnp.float32)).astype(jnp.bfloat16)


def times(table, values):
    high, low = halve(values)
    return dot(table[:, :256], high) + dot(table[:, 256:], high) + dot(table[:, :256], low)


def planes_kernel(left_ref, right_ref, left_up_ref, right_up_ref, z_ref, y_ref, out_ref):
    count = left_ref.shape[1]

    def field_grad(plane, parity, structure_ref, upstream_ref):
        rows = pl.ds(parity, half, stride=2)
        structure = structure_ref[0, plane, rows, :]
        return upstream_ref[0, plane, rows, :] * sigmoid_slope * structure * (1.0 - structure)

    def after_z(plane):
        field = jnp.concatenate(
            [
                jnp.concatenate(
                    (
                        field_grad(plane, parity, left_ref, left_up_ref),
                        field_grad(plane, parity, right_ref, right_up_ref),
                    ),
                    axis=1,
                )
                for parity in range(2)
            ],
            axis=0,
        )
        high, low = halve(field)
        return dot(high, z_ref[0:256]) + dot(low, z_ref[0:256]) + dot(high, z_ref[256:512])

    def after_y(values):
        sums = []
        for parity in range(2):
            rows = values[parity * half : (parity + 1) * half]
            stacked = jnp.concatenate((rows[:, :grid_length], rows[:, grid_length:]), axis=0)
            sums.append(times(y_ref[parity], stacked))
        return sums[0] + sums[1], sums[0] - sums[1]

    def store(plane, below, above):
        for part in range(2):
            rows = slice(part * half, (part + 1) * half)
            for side in range(2):
                lanes = slice(side * 128, (side + 1) * 128)
                out_ref[:16, side, part, 0, plane] = below[rows, lanes].reshape(16, 8, 128)
                out_ref[16:, side, part, 0, plane] = above[rows, lanes].reshape(16, 8, 128)

    pending = after_z(0)
    done = None
    for plane in range(count):
        following = after_z(plane + 1) if plane + 1 < count else None
        results = after_y(pending)
        if done is not None:
            store(plane - 1, *done)
        pending, done = following, results
    store(count - 1, *done)


planes_per_step = 4


def planes(structure, upstream):
    members, depth = structure.shape[:2]
    blocks = [
        pl.BlockSpec(
            (1, planes_per_step, grid_length, 128), lambda m, x, side=side: (m, x, 0, side)
        )
        for side in range(2)
    ]
    return pl.pallas_call(
        planes_kernel,
        out_shape=jax.ShapeDtypeStruct(
            (devices_slab, 2, 2, members, depth, 8, 128), jnp.float32
        ),
        grid=(members, depth // planes_per_step),
        in_specs=[
            *blocks,
            *blocks,
            pl.BlockSpec((512, 512), lambda m, x: (0, 0)),
            pl.BlockSpec((2, 256, 512), lambda m, x: (0, 0, 0)),
        ],
        out_specs=pl.BlockSpec(
            (devices_slab, 2, 2, 1, planes_per_step, 8, 128),
            lambda m, x: (0, 0, 0, m, x, 0, 0),
        ),
        compiler_params=pltpu.CompilerParams(vmem_limit_bytes=60 * 1024 * 1024),
        name="planes",
    )(structure, structure, upstream, upstream, along_z_table(), along_y_table())


def sums_kernel(
    side, core_ref, received_ref, noise_ref, x_ref, give_ref, keep_ref
):
    members = received_ref.shape[3]
    core = core_ref[0]
    noise = noise_ref.reshape(2, members, 4, 1024, 128)

    def spectra(m, pair):
        def samples(first, part, k):
            block = received_ref[first : first + 16, side, part, m, pl.ds(k, 8, stride=8), :]
            return block.reshape(half, 128)

        def stacked(sign):
            return jnp.concatenate(
                [
                    jnp.concatenate(
                        [
                            samples(0, part, 2 * pair + k) + sign * samples(16, part, 2 * pair + k)
                            for k in range(2)
                        ],
                        axis=1,
                    )
                    for part in range(2)
                ],
                axis=0,
            )

        return [times(x_ref[core, parity], stacked(1 - 2 * parity)) for parity in range(2)]

    def weighted(m, pair, pieces):
        for parity in range(2):
            for c, out_ref in enumerate((give_ref, keep_ref)):
                for z in range(2):
                    block = 2 * z + jnp.bitwise_xor(core, 1 - c)
                    start = 64 * c + 32 * z
                    for k in range(2):
                        lanes = slice(k * 128, (k + 1) * 128)
                        y = 2 * pair + k
                        rows = pl.ds(16 * parity + 8 * side + y, 32, stride=32)
                        value = (
                            noise[0, m, block, rows, :] * pieces[parity][start : start + 32, lanes]
                            + noise[1, m, block, rows, :]
                            * pieces[parity][half + start : half + start + 32, lanes]
                        )
                        if m > 0:
                            value = value + out_ref[z, parity, y]
                        out_ref[z, parity, y] = value

    steps = [(m, pair) for m in range(members) for pair in range(4)]
    pieces = spectra(*steps[0])
    for i, (m, pair) in enumerate(steps):
        following = spectra(*steps[i + 1]) if i + 1 < len(steps) else None
        weighted(m, pair, pieces)
        pieces = following


def sums(side, received, noise, core):
    members = received.shape[3]
    out = jax.ShapeDtypeStruct((2, 2, 8, 32, 128), jnp.float32)
    vmem = pl.BlockSpec(memory_space=pltpu.VMEM)
    return pl.pallas_call(
        functools.partial(sums_kernel, side),
        out_shape=(out, out),
        in_specs=[
            pl.BlockSpec(memory_space=pltpu.SMEM),
            vmem,
            vmem,
            vmem,
        ],
        out_specs=(vmem, vmem),
        compiler_params=pltpu.CompilerParams(vmem_limit_bytes=24 * 1024 * 1024),
        name="sums",
    )(
        core,
        received.reshape(devices_slab, 2, 2, members, 64, 128),
        noise,
        along_x_table(),
    )


def density_kernel(z_ref, *refs):
    z = z_ref[0]
    density_ref, out_ref = refs[6], refs[7]
    density = density_ref.reshape(1024, 128)
    out = out_ref.reshape(1024, 128)
    for side in range(2):
        ours, chip, theirs = refs[3 * side : 3 * side + 3]
        for parity in range(2):
            for y in range(8):
                rows = pl.ds(16 * parity + 8 * side + y, 32, stride=32)
                total = ours[z, parity, y] + chip[z, parity, y] + theirs[parity, y]
                out[rows, :] = total / (2.0 * jnp.sqrt(density[rows, :]))


def tiles(values):
    values = values.reshape(values.shape[:-1] + (2, 128))
    return jnp.swapaxes(values, -3, -2)


def untiles(values):
    values = jnp.swapaxes(values, -3, -2)
    return values.reshape(values.shape[:-2] + (grid_length,))


def density_gradient(z_lo, pieces, density):
    vmem = pl.BlockSpec(memory_space=pltpu.VMEM)
    result = pl.pallas_call(
        density_kernel,
        out_shape=jax.ShapeDtypeStruct((64, 2, 8, 128), jnp.float32),
        in_specs=[pl.BlockSpec(memory_space=pltpu.SMEM)] + [vmem] * 7,
        out_specs=vmem,
        compiler_params=pltpu.CompilerParams(vmem_limit_bytes=8 * 1024 * 1024),
        name="density",
    )(z_lo, *pieces, tiles(density))
    return untiles(result)


def swap(values, flip):
    return lax.ppermute(values, "member", [(i, i ^ flip) for i in range(devices_member)])


def body(structure, upstream, noise, density):
    index = lax.axis_index("member").astype(jnp.int32)
    z_lo, core = index // 2, index % 2
    sent = planes(structure, upstream)
    sent, z_lo, core = lax.optimization_barrier((sent, z_lo, core))
    received = lax.all_to_all(sent, "slab", split_axis=0, concat_axis=0, tiled=True)
    received, z_lo, core = lax.optimization_barrier((received, z_lo, core))
    members = structure.shape[0]
    noise = tiles(noise).reshape(2, members, 4, 64, 2, 8, 128)
    pieces = []
    for side in range(2):
        give, keep = sums(side, received, noise, core.reshape(1))
        from_core = swap(give, 1)
        onward = lax.dynamic_index_in_dim(from_core, 1 - z_lo, 0, keepdims=False)
        onward = onward + lax.dynamic_index_in_dim(keep, 1 - z_lo, 0, keepdims=False)
        pieces += [keep, from_core, swap(onward, 2)]
    return density_gradient(z_lo.reshape(1), pieces, density)


def solution(mesh):
    in_specs = (
        P("member", "slab", None, None),
        P("member", "slab", None, None),
        P(None, "member", None, "slab", None),
        P("member", "slab", None),
    )
    out_specs = P("member", "slab", None)
    return jax.shard_map(body, mesh=mesh, in_specs=in_specs, out_specs=out_specs, check_vma=False)
```

```python
import functools
import math

import jax
import jax.numpy as jnp
import ml_dtypes
import numpy as np
from jax import lax
from jax.experimental import pallas as pl
from jax.experimental.pallas import tpu as pltpu
from jax.sharding import PartitionSpec as P

sigmoid_slope = 8.0
grid_length = 256
half = grid_length // 2
devices_slab = 32
devices_member = 4


def waves(rows, columns):
    angles = (np.outer(rows, columns) % grid_length) * (2.0 * math.pi / grid_length)
    return np.cos(angles) / 16.0, -np.sin(angles) / 16.0


def split_table(table):
    high = table.astype(np.float32).astype(ml_dtypes.bfloat16)
    low = (table - high.astype(np.float64)).astype(np.float32).astype(ml_dtypes.bfloat16)
    return high, low


def along_z_table():
    real, imag = waves(np.arange(grid_length), np.arange(grid_length))
    high, low = split_table(np.concatenate((real, imag), axis=1))
    return np.concatenate((high, low), axis=0)


def stacked_table(real, imag):
    full = np.concatenate(
        (np.concatenate((real, -imag), axis=1), np.concatenate((imag, real), axis=1)), axis=0
    )
    return np.concatenate(split_table(full), axis=1)


def along_y_table():
    return np.stack(
        [
            stacked_table(*waves(np.arange(half), np.arange(parity, grid_length, 2)))
            for parity in range(2)
        ]
    )


def along_x_table():
    return np.stack(
        [
            np.stack(
                [
                    stacked_table(*waves(2 * np.arange(32 * i, 32 * i + 32) + parity, np.arange(half)))
                    for parity in range(2)
                ]
            )
            for i in range(devices_member)
        ]
    )


def dot(left, right):
    return jnp.dot(left, right, preferred_element_type=jnp.float32)


def halve(values):
    high = values.astype(jnp.bfloat16)
    return high, (values - high.astype(jnp.float32)).astype(jnp.bfloat16)


def times(table, values):
    high, low = halve(values)
    return dot(table[:, :256], high) + dot(table[:, 256:], high) + dot(table[:, :256], low)


def planes_kernel(left_ref, right_ref, left_up_ref, right_up_ref, z_ref, y_ref, out_ref):
    count = left_ref.shape[1]

    def field_grad(plane, parity, structure_ref, upstream_ref):
        rows = pl.ds(parity, half, stride=2)
        structure = structure_ref[0, plane, rows, :]
        return upstream_ref[0, plane, rows, :] * sigmoid_slope * structure * (1.0 - structure)

    def after_z(plane):
        field = jnp.concatenate(
            [
                jnp.concatenate(
                    (
                        field_grad(plane, parity, left_ref, left_up_ref),
                        field_grad(plane, parity, right_ref, right_up_ref),
                    ),
                    axis=1,
                )
                for parity in range(2)
            ],
            axis=0,
        )
        high, low = halve(field)
        return dot(high, z_ref[0:256]) + dot(low, z_ref[0:256]) + dot(high, z_ref[256:512])

    def after_y(values):
        sums = []
        for parity in range(2):
            rows = values[parity * half : (parity + 1) * half]
            stacked = jnp.concatenate((rows[:, :grid_length], rows[:, grid_length:]), axis=0)
            sums.append(times(y_ref[parity], stacked))
        return sums[0] + sums[1], sums[0] - sums[1]

    def store(plane, below, above):
        for part in range(2):
            rows = slice(part * half, (part + 1) * half)
            for side in range(2):
                lanes = slice(side * 128, (side + 1) * 128)
                out_ref[:16, side, part, 0, plane] = below[rows, lanes].reshape(16, 8, 128)
                out_ref[16:, side, part, 0, plane] = above[rows, lanes].reshape(16, 8, 128)

    pending = after_z(0)
    done = None
    for plane in range(count):
        following = after_z(plane + 1) if plane + 1 < count else None
        results = after_y(pending)
        if done is not None:
            store(plane - 1, *done)
        pending, done = following, results
    store(count - 1, *done)


planes_per_step = 4


def planes(structure, upstream):
    members, depth = structure.shape[:2]
    blocks = [
        pl.BlockSpec(
            (1, planes_per_step, grid_length, 128), lambda m, x, side=side: (m, x, 0, side)
        )
        for side in range(2)
    ]
    return pl.pallas_call(
        planes_kernel,
        out_shape=jax.ShapeDtypeStruct(
            (devices_slab, 2, 2, members, depth, 8, 128), jnp.float32
        ),
        grid=(members, depth // planes_per_step),
        in_specs=[
            *blocks,
            *blocks,
            pl.BlockSpec((512, 512), lambda m, x: (0, 0)),
            pl.BlockSpec((2, 256, 512), lambda m, x: (0, 0, 0)),
        ],
        out_specs=pl.BlockSpec(
            (devices_slab, 2, 2, 1, planes_per_step, 8, 128),
            lambda m, x: (0, 0, 0, m, x, 0, 0),
        ),
        compiler_params=pltpu.CompilerParams(vmem_limit_bytes=60 * 1024 * 1024),
        name="planes",
    )(structure, structure, upstream, upstream, along_z_table(), along_y_table())


def sums_kernel(sides, place_ref, received_ref, noise_ref, x_ref, give_ref, keep_ref):
    members = received_ref.shape[3]
    noise = noise_ref.reshape(2, members, devices_member, 1024, 128)
    give, keep = 2 * place_ref[0] + 1 - place_ref[1], 2 * place_ref[0] + place_ref[1]
    outputs = ((give, give_ref), (keep, keep_ref))
    tables = [
        jnp.concatenate([x_ref[block, parity] for block, _ in outputs], axis=0)
        for parity in range(2)
    ]

    def spectra(side, m, pair):
        def samples(first, part, k):
            block = received_ref[first : first + 16, side, part, m, pl.ds(k, 8, stride=8), :]
            return block.reshape(half, 128)

        def stacked(sign):
            return jnp.concatenate(
                [
                    jnp.concatenate(
                        [
                            samples(0, part, 2 * pair + k) + sign * samples(16, part, 2 * pair + k)
                            for k in range(2)
                        ],
                        axis=1,
                    )
                    for part in range(2)
                ],
                axis=0,
            )

        return [times(tables[parity], stacked(1 - 2 * parity)) for parity in range(2)]

    def weighted(side, m, pair, pieces, earlier):
        values = {}
        for parity in range(2):
            for i, (block, _) in enumerate(outputs):
                for k in range(2):
                    lanes = slice(k * 128, (k + 1) * 128)
                    y = 2 * pair + k
                    rows = pl.ds(16 * parity + 8 * side + y, 32, stride=32)
                    value = (
                        noise[0, m, block, rows, :] * pieces[parity][64 * i : 64 * i + 32, lanes]
                        + noise[1, m, block, rows, :]
                        * pieces[parity][64 * i + 32 : 64 * i + 64, lanes]
                    )
                    key = (i, parity, y)
                    values[key] = value + earlier[key] if earlier else value
        return values

    for position, side in enumerate(sides):
        for pair in range(4):
            values = None
            for m in range(members):
                values = weighted(side, m, pair, spectra(side, m, pair), values)
            for (i, parity, y), value in values.items():
                rows = pl.ds(8 * parity + y, 32, stride=16)
                outputs[i][1].at[position].reshape(512, 128)[rows, :] = value


def sums(sides, received, noise, place):
    members = received.shape[3]
    out = jax.ShapeDtypeStruct((len(sides), 64, 8, 128), jnp.float32)
    vmem = pl.BlockSpec(memory_space=pltpu.VMEM)
    return pl.pallas_call(
        functools.partial(sums_kernel, sides),
        out_shape=(out, out),
        in_specs=[pl.BlockSpec(memory_space=pltpu.SMEM), vmem, vmem, vmem],
        out_specs=(vmem, vmem),
        compiler_params=pltpu.CompilerParams(vmem_limit_bytes=24 * 1024 * 1024),
        cost_estimate=pl.CostEstimate(
            flops=len(sides) * 6 * members * 16 * 128 * 256 * 256,
            bytes_accessed=len(sides) * 16 * 1024 * 1024,
            transcendentals=0,
        ),
        name="sums",
    )(
        place,
        received.reshape(devices_slab, 2, 2, members, 64, 128),
        noise,
        along_x_table(),
    )


def tiles(values):
    values = values.reshape(values.shape[:-1] + (2, 128))
    return jnp.swapaxes(values, -3, -2)


def untiles(values):
    values = jnp.swapaxes(values, -3, -2)
    return values.reshape(values.shape[:-2] + (grid_length,))


def swap(values, flip):
    return lax.ppermute(values, "member", [(i, i ^ flip) for i in range(devices_member)])


def body(structure, upstream, noise, density):
    index = lax.axis_index("member").astype(jnp.int32)
    z_lo, core = index // 2, index % 2
    ours, theirs = jnp.stack((z_lo, core)), jnp.stack((1 - z_lo, core))
    sent = planes(structure, upstream)
    sent, ours, theirs = lax.optimization_barrier((sent, ours, theirs))
    received = lax.all_to_all(sent, "slab", split_axis=0, concat_axis=0, tiled=True)
    received, ours, theirs = lax.optimization_barrier((received, ours, theirs))
    noise = tiles(noise).reshape(2, structure.shape[0], devices_member, 64, 2, 8, 128)
    crossing = []
    for side in range(2):
        give, keep = sums((side,), received, noise, theirs)
        crossing.append(swap(give, 1) + keep)
    crossing = jnp.concatenate(crossing)
    arrived = swap(crossing, 2)
    ours, _ = lax.optimization_barrier((ours, crossing))
    give, keep = sums((0, 1), received, noise, ours)
    chip = jnp.concatenate([swap(give[side : side + 1], 1) for side in range(2)])
    total = keep + chip + arrived
    return untiles(jnp.swapaxes(total, 0, 1) / (2.0 * jnp.sqrt(tiles(density))))


def solution(mesh):
    in_specs = (
        P("member", "slab", None, None),
        P("member", "slab", None, None),
        P(None, "member", None, "slab", None),
        P("member", "slab", None),
    )
    out_specs = P("member", "slab", None)
    return jax.shard_map(body, mesh=mesh, in_specs=in_specs, out_specs=out_specs, check_vma=False)
```

```python
import functools
import math

import jax
import jax.numpy as jnp
import ml_dtypes
import numpy as np
from jax import lax
from jax.experimental import pallas as pl
from jax.experimental.pallas import tpu as pltpu
from jax.sharding import PartitionSpec as P

sigmoid_slope = 8.0
grid_length = 256
half = grid_length // 2
devices_slab = 32
devices_member = 4


def waves(rows, columns):
    angles = (np.outer(rows, columns) % grid_length) * (2.0 * math.pi / grid_length)
    return np.cos(angles) / 16.0, -np.sin(angles) / 16.0


def split_table(table):
    high = table.astype(np.float32).astype(ml_dtypes.bfloat16)
    low = (table - high.astype(np.float64)).astype(np.float32).astype(ml_dtypes.bfloat16)
    return high, low


def along_z_table():
    real, imag = waves(np.arange(grid_length), np.arange(half + 1))
    high, low = split_table(np.concatenate((real[:, :half], real[:, half:], imag[:, 1:half]), axis=1))
    return np.concatenate((high, low), axis=0)


def stacked_table(real, imag):
    full = np.concatenate(
        (np.concatenate((real, -imag), axis=1), np.concatenate((imag, real), axis=1)), axis=0
    )
    return np.concatenate(split_table(full), axis=1)


def along_y_table():
    return np.stack(
        [
            stacked_table(*waves(np.arange(half), np.arange(parity, grid_length, 2)))
            for parity in range(2)
        ]
    )


def along_x_table():
    return np.stack(
        [
            np.stack(
                [
                    stacked_table(*waves(2 * np.arange(32 * i, 32 * i + 32) + parity, np.arange(half)))
                    for parity in range(2)
                ]
            )
            for i in range(devices_member)
        ]
    )


def dot(left, right):
    return jnp.dot(left, right, preferred_element_type=jnp.float32)


def halve(values):
    high = values.astype(jnp.bfloat16)
    return high, (values - high.astype(jnp.float32)).astype(jnp.bfloat16)


def times(table, values):
    high, low = halve(values)
    return dot(table[:, :256], high) + dot(table[:, 256:], high) + dot(table[:, :256], low)


def planes_kernel(left_ref, right_ref, left_up_ref, right_up_ref, z_ref, y_ref, out_ref):
    count = left_ref.shape[1]

    def field_grad(plane, parity, structure_ref, upstream_ref):
        rows = pl.ds(parity, half, stride=2)
        structure = structure_ref[0, plane, rows, :]
        return upstream_ref[0, plane, rows, :] * sigmoid_slope * structure * (1.0 - structure)

    def after_z(plane):
        field = jnp.concatenate(
            [
                jnp.concatenate(
                    (
                        field_grad(plane, parity, left_ref, left_up_ref),
                        field_grad(plane, parity, right_ref, right_up_ref),
                    ),
                    axis=1,
                )
                for parity in range(2)
            ],
            axis=0,
        )
        high, low = halve(field)
        table_high, table_low = z_ref[0:256], z_ref[256:512]
        raw = dot(high, table_high) + dot(low, table_high) + dot(high, table_low)
        below_real, below_imag = raw[:, :half], raw[:, half:]
        lane = lax.broadcasted_iota(jnp.int32, (grid_length, half), 1)
        first = lane == 0
        opposite = jnp.where(first, 0, half - lane)

        def mirrored(values):
            return jnp.take_along_axis(values, opposite, axis=1, mode="promise_in_bounds")

        above_real = jnp.where(first, below_imag, mirrored(below_real))
        above_imag = jnp.where(first, 0.0, -mirrored(below_imag))
        below_imag = jnp.where(first, 0.0, below_imag)
        return jnp.concatenate((below_real, above_real, below_imag, above_imag), axis=1)

    def after_y(values):
        sums = []
        for parity in range(2):
            rows = values[parity * half : (parity + 1) * half]
            stacked = jnp.concatenate((rows[:, :grid_length], rows[:, grid_length:]), axis=0)
            sums.append(times(y_ref[parity], stacked))
        return sums[0] + sums[1], sums[0] - sums[1]

    def store(plane, below, above):
        for part in range(2):
            rows = slice(part * half, (part + 1) * half)
            for side in range(2):
                lanes = slice(side * 128, (side + 1) * 128)
                out_ref[:16, side, part, 0, plane] = below[rows, lanes].reshape(16, 8, 128)
                out_ref[16:, side, part, 0, plane] = above[rows, lanes].reshape(16, 8, 128)

    pending = after_z(0)
    done = None
    for plane in range(count):
        following = after_z(plane + 1) if plane + 1 < count else None
        results = after_y(pending)
        if done is not None:
            store(plane - 1, *done)
        pending, done = following, results
    store(count - 1, *done)


planes_per_step = 4


def planes(structure, upstream):
    members, depth = structure.shape[:2]
    blocks = [
        pl.BlockSpec(
            (1, planes_per_step, grid_length, 128), lambda m, x, side=side: (m, x, 0, side)
        )
        for side in range(2)
    ]
    return pl.pallas_call(
        planes_kernel,
        out_shape=jax.ShapeDtypeStruct(
            (devices_slab, 2, 2, members, depth, 8, 128), jnp.float32
        ),
        grid=(members, depth // planes_per_step),
        in_specs=[
            *blocks,
            *blocks,
            pl.BlockSpec((512, 256), lambda m, x: (0, 0)),
            pl.BlockSpec((2, 256, 512), lambda m, x: (0, 0, 0)),
        ],
        out_specs=pl.BlockSpec(
            (devices_slab, 2, 2, 1, planes_per_step, 8, 128),
            lambda m, x: (0, 0, 0, m, x, 0, 0),
        ),
        compiler_params=pltpu.CompilerParams(vmem_limit_bytes=60 * 1024 * 1024),
        name="planes",
    )(structure, structure, upstream, upstream, along_z_table(), along_y_table())


def sums_kernel(sides, place_ref, received_ref, noise_ref, x_ref, give_ref, keep_ref):
    members = received_ref.shape[3]
    noise = noise_ref.reshape(2, members, devices_member, 1024, 128)
    give, keep = 2 * place_ref[0] + 1 - place_ref[1], 2 * place_ref[0] + place_ref[1]
    outputs = ((give, give_ref), (keep, keep_ref))
    tables = [
        jnp.concatenate([x_ref[block, parity] for block, _ in outputs], axis=0)
        for parity in range(2)
    ]

    def spectra(side, m, pair):
        def samples(first, part, k):
            block = received_ref[first : first + 16, side, part, m, pl.ds(k, 8, stride=8), :]
            return block.reshape(half, 128)

        def stacked(sign):
            return jnp.concatenate(
                [
                    jnp.concatenate(
                        [
                            samples(0, part, 2 * pair + k) + sign * samples(16, part, 2 * pair + k)
                            for k in range(2)
                        ],
                        axis=1,
                    )
                    for part in range(2)
                ],
                axis=0,
            )

        return [times(tables[parity], stacked(1 - 2 * parity)) for parity in range(2)]

    def weighted(side, m, pair, pieces, earlier):
        values = {}
        for parity in range(2):
            for i, (block, _) in enumerate(outputs):
                for k in range(2):
                    lanes = slice(k * 128, (k + 1) * 128)
                    y = 2 * pair + k
                    rows = pl.ds(16 * parity + 8 * side + y, 32, stride=32)
                    value = (
                        noise[0, m, block, rows, :] * pieces[parity][64 * i : 64 * i + 32, lanes]
                        + noise[1, m, block, rows, :]
                        * pieces[parity][64 * i + 32 : 64 * i + 64, lanes]
                    )
                    key = (i, parity, y)
                    values[key] = value + earlier[key] if earlier else value
        return values

    for position, side in enumerate(sides):
        for pair in range(4):
            values = None
            for m in range(members):
                values = weighted(side, m, pair, spectra(side, m, pair), values)
            for (i, parity, y), value in values.items():
                rows = pl.ds(8 * parity + y, 32, stride=16)
                outputs[i][1].at[position].reshape(512, 128)[rows, :] = value


def sums(sides, received, noise, place):
    members = received.shape[3]
    out = jax.ShapeDtypeStruct((len(sides), 64, 8, 128), jnp.float32)
    vmem = pl.BlockSpec(memory_space=pltpu.VMEM)
    return pl.pallas_call(
        functools.partial(sums_kernel, sides),
        out_shape=(out, out),
        in_specs=[pl.BlockSpec(memory_space=pltpu.SMEM), vmem, vmem, vmem],
        out_specs=(vmem, vmem),
        compiler_params=pltpu.CompilerParams(vmem_limit_bytes=24 * 1024 * 1024),
        cost_estimate=pl.CostEstimate(
            flops=len(sides) * 6 * members * 16 * 128 * 256 * 256,
            bytes_accessed=len(sides) * 16 * 1024 * 1024,
            transcendentals=0,
        ),
        name="sums",
    )(
        place,
        received.reshape(devices_slab, 2, 2, members, 64, 128),
        noise,
        along_x_table(),
    )


def tiles(values):
    values = values.reshape(values.shape[:-1] + (2, 128))
    return jnp.swapaxes(values, -3, -2)


def untiles(values):
    values = jnp.swapaxes(values, -3, -2)
    return values.reshape(values.shape[:-2] + (grid_length,))


def swap(values, flip):
    return lax.ppermute(values, "member", [(i, i ^ flip) for i in range(devices_member)])


def body(structure, upstream, noise, density):
    index = lax.axis_index("member").astype(jnp.int32)
    z_lo, core = index // 2, index % 2
    ours, theirs = jnp.stack((z_lo, core)), jnp.stack((1 - z_lo, core))
    sent = planes(structure, upstream)
    sent, ours, theirs = lax.optimization_barrier((sent, ours, theirs))
    received = lax.all_to_all(sent, "slab", split_axis=0, concat_axis=0, tiled=True)
    received, ours, theirs = lax.optimization_barrier((received, ours, theirs))
    noise = tiles(noise).reshape(2, structure.shape[0], devices_member, 64, 2, 8, 128)
    give, keep = sums((0, 1), received, noise, theirs)
    crossing = swap(give, 1) + keep
    arrived = swap(crossing, 2)
    ours, _ = lax.optimization_barrier((ours, crossing))
    give, keep = sums((0, 1), received, noise, ours)
    chip = jnp.concatenate([swap(give[side : side + 1], 1) for side in range(2)])
    total = keep + chip + arrived
    return untiles(jnp.swapaxes(total, 0, 1) / (2.0 * jnp.sqrt(tiles(density))))


def solution(mesh):
    in_specs = (
        P("member", "slab", None, None),
        P("member", "slab", None, None),
        P(None, "member", None, "slab", None),
        P("member", "slab", None),
    )
    out_specs = P("member", "slab", None)
    return jax.shard_map(body, mesh=mesh, in_specs=in_specs, out_specs=out_specs, check_vma=False)
```

```python
import functools
import math

import jax
import jax.numpy as jnp
import ml_dtypes
import numpy as np
from jax import lax
from jax.experimental import pallas as pl
from jax.experimental.pallas import tpu as pltpu
from jax.sharding import PartitionSpec as P

sigmoid_slope = 8.0
grid_length = 256
half = grid_length // 2
devices_slab = 32
devices_member = 4


def waves(rows, columns):
    angles = (np.outer(rows, columns) % grid_length) * (2.0 * math.pi / grid_length)
    return np.cos(angles) / 16.0, -np.sin(angles) / 16.0


def split_table(table):
    high = table.astype(np.float32).astype(ml_dtypes.bfloat16)
    low = (table - high.astype(np.float64)).astype(np.float32).astype(ml_dtypes.bfloat16)
    return high, low


def along_z_table():
    real, imag = waves(np.arange(grid_length), np.arange(half + 1))
    high, low = split_table(np.concatenate((real[:, :half], real[:, half:], imag[:, 1:half]), axis=1))
    return np.concatenate((high, low), axis=0)


def stacked_table(real, imag):
    full = np.concatenate(
        (np.concatenate((real, -imag), axis=1), np.concatenate((imag, real), axis=1)), axis=0
    )
    return np.concatenate(split_table(full), axis=1)


def along_y_table():
    return np.stack(
        [
            stacked_table(*waves(np.arange(half), np.arange(parity, grid_length, 2)))
            for parity in range(2)
        ]
    )


def along_x_table():
    return np.stack(
        [
            np.stack(
                [
                    stacked_table(*waves(2 * np.arange(32 * i, 32 * i + 32) + parity, np.arange(half)))
                    for parity in range(2)
                ]
            )
            for i in range(devices_member)
        ]
    )


def dot(left, right):
    return jnp.dot(left, right, preferred_element_type=jnp.float32)


def halve(values):
    high = values.astype(jnp.bfloat16)
    return high, (values - high.astype(jnp.float32)).astype(jnp.bfloat16)


def times(table, values):
    high, low = halve(values)
    rows = table.shape[0]
    both = dot(jnp.concatenate((table[:, :256], table[:, 256:]), axis=0), high)
    return both[:rows] + both[rows:] + dot(table[:, :256], low)


def planes_kernel(left_ref, right_ref, left_up_ref, right_up_ref, z_ref, y_ref, out_ref):
    count = left_ref.shape[1]

    def field_grad(plane, parity, structure_ref, upstream_ref):
        rows = pl.ds(parity, half, stride=2)
        structure = structure_ref[0, plane, rows, :]
        return upstream_ref[0, plane, rows, :] * sigmoid_slope * structure * (1.0 - structure)

    def after_z(plane):
        field = jnp.concatenate(
            [
                jnp.concatenate(
                    (
                        field_grad(plane, parity, left_ref, left_up_ref),
                        field_grad(plane, parity, right_ref, right_up_ref),
                    ),
                    axis=1,
                )
                for parity in range(2)
            ],
            axis=0,
        )
        high, low = halve(field)
        table_high, table_low = z_ref[0:256], z_ref[256:512]
        raw = dot(high, table_high) + dot(low, table_high) + dot(high, table_low)
        below_real, below_imag = raw[:, :half], raw[:, half:]
        lane = lax.broadcasted_iota(jnp.int32, (grid_length, half), 1)
        first = lane == 0
        opposite = jnp.where(first, 0, half - lane)

        def mirrored(values):
            return jnp.take_along_axis(values, opposite, axis=1, mode="promise_in_bounds")

        above_real = jnp.where(first, below_imag, mirrored(below_real))
        above_imag = jnp.where(first, 0.0, -mirrored(below_imag))
        below_imag = jnp.where(first, 0.0, below_imag)
        return jnp.concatenate((below_real, above_real, below_imag, above_imag), axis=1)

    def after_y(values):
        sums = []
        for parity in range(2):
            rows = values[parity * half : (parity + 1) * half]
            stacked = jnp.concatenate((rows[:, :grid_length], rows[:, grid_length:]), axis=0)
            sums.append(times(y_ref[parity], stacked))
        return sums[0] + sums[1], sums[0] - sums[1]

    def store(plane, below, above):
        for part in range(2):
            rows = slice(part * half, (part + 1) * half)
            for side in range(2):
                lanes = slice(side * 128, (side + 1) * 128)
                out_ref[:16, side, part, 0, plane] = below[rows, lanes].reshape(16, 8, 128)
                out_ref[16:, side, part, 0, plane] = above[rows, lanes].reshape(16, 8, 128)

    pending = after_z(0)
    done = None
    for plane in range(count):
        following = after_z(plane + 1) if plane + 1 < count else None
        results = after_y(pending)
        if done is not None:
            store(plane - 1, *done)
        pending, done = following, results
    store(count - 1, *done)


planes_per_step = 4


def planes(structure, upstream):
    members, depth = structure.shape[:2]
    blocks = [
        pl.BlockSpec(
            (1, planes_per_step, grid_length, 128), lambda m, x, side=side: (m, x, 0, side)
        )
        for side in range(2)
    ]
    return pl.pallas_call(
        planes_kernel,
        out_shape=jax.ShapeDtypeStruct(
            (devices_slab, 2, 2, members, depth, 8, 128), jnp.float32
        ),
        grid=(members, depth // planes_per_step),
        in_specs=[
            *blocks,
            *blocks,
            pl.BlockSpec((512, 256), lambda m, x: (0, 0)),
            pl.BlockSpec((2, 256, 512), lambda m, x: (0, 0, 0)),
        ],
        out_specs=pl.BlockSpec(
            (devices_slab, 2, 2, 1, planes_per_step, 8, 128),
            lambda m, x: (0, 0, 0, m, x, 0, 0),
        ),
        compiler_params=pltpu.CompilerParams(vmem_limit_bytes=60 * 1024 * 1024),
        name="planes",
    )(structure, structure, upstream, upstream, along_z_table(), along_y_table())


def sums_kernel(sides, place_ref, received_ref, noise_ref, x_ref, give_ref, keep_ref):
    members = received_ref.shape[3]
    noise = noise_ref.reshape(2, members, devices_member, 1024, 128)
    give, keep = 2 * place_ref[0] + 1 - place_ref[1], 2 * place_ref[0] + place_ref[1]
    outputs = ((give, give_ref), (keep, keep_ref))
    tables = [
        jnp.concatenate([x_ref[block, parity] for block, _ in outputs], axis=0)
        for parity in range(2)
    ]

    def spectra(side, m, pair):
        def samples(first, part, k):
            block = received_ref[first : first + 16, side, part, m, pl.ds(k, 8, stride=8), :]
            return block.reshape(half, 128)

        def stacked(first):
            return jnp.concatenate(
                [
                    jnp.concatenate([samples(first, part, 2 * pair + k) for k in range(2)], axis=1)
                    for part in range(2)
                ],
                axis=0,
            )

        low, high = stacked(0), stacked(16)
        return times(tables[0], low + high), times(tables[1], low - high)

    def weighted(side, m, pair, pieces, earlier):
        values = {}
        for parity in range(2):
            for i, (block, _) in enumerate(outputs):
                for k in range(2):
                    lanes = slice(k * 128, (k + 1) * 128)
                    y = 2 * pair + k
                    rows = pl.ds(16 * parity + 8 * side + y, 32, stride=32)
                    value = (
                        noise[0, m, block, rows, :] * pieces[parity][64 * i : 64 * i + 32, lanes]
                        + noise[1, m, block, rows, :]
                        * pieces[parity][64 * i + 32 : 64 * i + 64, lanes]
                    )
                    key = (i, parity, y)
                    values[key] = value + earlier[key] if earlier else value
        return values

    for position, side in enumerate(sides):
        for pair in range(4):
            values = None
            for m in range(members):
                values = weighted(side, m, pair, spectra(side, m, pair), values)
            for (i, parity, y), value in values.items():
                rows = pl.ds(8 * parity + y, 32, stride=16)
                outputs[i][1].at[position].reshape(512, 128)[rows, :] = value


def sums(sides, received, noise, place):
    members = received.shape[3]
    out = jax.ShapeDtypeStruct((len(sides), 64, 8, 128), jnp.float32)
    vmem = pl.BlockSpec(memory_space=pltpu.VMEM)
    return pl.pallas_call(
        functools.partial(sums_kernel, sides),
        out_shape=(out, out),
        in_specs=[pl.BlockSpec(memory_space=pltpu.SMEM), vmem, vmem, vmem],
        out_specs=(vmem, vmem),
        compiler_params=pltpu.CompilerParams(vmem_limit_bytes=24 * 1024 * 1024),
        cost_estimate=pl.CostEstimate(
            flops=len(sides) * 6 * members * 16 * 128 * 256 * 256,
            bytes_accessed=len(sides) * 16 * 1024 * 1024,
            transcendentals=0,
        ),
        name="sums",
    )(
        place,
        received.reshape(devices_slab, 2, 2, members, 64, 128),
        noise,
        along_x_table(),
    )


def tiles(values):
    values = values.reshape(values.shape[:-1] + (2, 128))
    return jnp.swapaxes(values, -3, -2)


def untiles(values):
    values = jnp.swapaxes(values, -3, -2)
    return values.reshape(values.shape[:-2] + (grid_length,))


def swap(values, flip):
    return lax.ppermute(values, "member", [(i, i ^ flip) for i in range(devices_member)])


def body(structure, upstream, noise, density):
    index = lax.axis_index("member").astype(jnp.int32)
    z_lo, core = index // 2, index % 2
    ours, theirs = jnp.stack((z_lo, core)), jnp.stack((1 - z_lo, core))
    sent = planes(structure, upstream)
    sent, ours, theirs = lax.optimization_barrier((sent, ours, theirs))
    received = lax.all_to_all(sent, "slab", split_axis=0, concat_axis=0, tiled=True)
    received, ours, theirs = lax.optimization_barrier((received, ours, theirs))
    noise = tiles(noise).reshape(2, structure.shape[0], devices_member, 64, 2, 8, 128)
    give, keep = sums((0, 1), received, noise, theirs)
    crossing = swap(give, 1) + keep
    arrived = swap(crossing, 2)
    ours, _ = lax.optimization_barrier((ours, crossing))
    give, keep = sums((0, 1), received, noise, ours)
    chip = jnp.concatenate([swap(give[side : side + 1], 1) for side in range(2)])
    total = keep + chip + arrived
    return untiles(jnp.swapaxes(total, 0, 1) / (2.0 * jnp.sqrt(tiles(density))))


def solution(mesh):
    in_specs = (
        P("member", "slab", None, None),
        P("member", "slab", None, None),
        P(None, "member", None, "slab", None),
        P("member", "slab", None),
    )
    out_specs = P("member", "slab", None)
    return jax.shard_map(body, mesh=mesh, in_specs=in_specs, out_specs=out_specs, check_vma=False)
```
